32 devices in a mesh: groups: 2 (over y), tensor: 4 (over z), dp: 4 (over x, core).
Axes of the slice: x: 2, y: 2, z: 4, core: 2. Of those that a mesh axis runs over, the one named last changes fastest.
Arguments:
- hidden: bfloat16 [2048, 53248], P(('groups', 'dp'), 'tensor'), parts along dimension 0, may hold values from -6 to 6
- down_weight: bfloat16 [53248, 8192], P('tensor', 'dp'), may hold values from -0.02734375 to 0.02734375
- scales: bfloat16 [8192], replicated, may hold values from 0.29882812 to 3
- residual: bfloat16 [2048, 8192], P('groups', ('dp', 'tensor')), parts along dimension 0, may hold values from -6 to 6
Outputs:
- updated: bfloat16 [2048, 8192], P('groups', ('dp', 'tensor')), parts along dimension 0
The draws below stay inside these ranges and needn't reach their ends.
There are 2 independent parts, one for each index of `groups`. The reference program is written for one: setup_inputs(seed, part) draws one part's arguments, and reference() takes and returns one part's arrays. A program takes and returns all parts, laid end to end along the dimension named above; an argument that names none is the same for every part. Nothing has to cross between parts.
All inputs are finite; a program needn't handle non-finite values.
Results may differ from the reference program's by a relative error of at most 0.0046.
Values may be sent and summed in bfloat16 or wider, within the bound.
A program may use at most 256 MiB of HBM per device.

```python
import math
import jax
import jax.numpy as jnp
from jax import lax

D = 8192
FF = 53248
LH = 64
TOKENS = 1024
N_TENSOR = 4


def block_scale(key, extent, split, low, top_value):
    level, own = 1.0, jax.random.fold_in(key, 6)
    for dim, blocks in split:
        draws = jnp.exp(jax.random.uniform(jax.random.fold_in(own, dim), (blocks,), jnp.float32, low / len(split), top_value / len(split)))
        level = level * jnp.repeat(draws, extent[dim] // blocks).reshape([-1 if axis == dim else 1 for axis in range(len(extent))])
    return level


def bell_draw(key, shape, deviation, bound, cuts=(), kind=jnp.bfloat16):
    level = block_scale(key, shape, cuts, -0.22, 0.18) if cuts else 1.0
    result = jax.random.normal(key, shape, jnp.float32) * deviation * level
    return jnp.minimum(jnp.maximum(result, -bound), bound).astype(kind)


def setup_inputs(seed: int = 0, part: int = 0) -> dict:
    streams_of = jax.random.split(jax.random.key(seed), 5)
    own_keys = jax.random.split(jax.random.fold_in(streams_of[4], part), 5)
    hidden = bell_draw(own_keys[0], (TOKENS, FF), 1.0, 6.0, ((0, 4), (1, 4)))
    down_weight = bell_draw(streams_of[1], (FF, D), FF ** -0.5, 0.02734375, ((0, 4), (1, 4)))
    scales = jnp.clip(jnp.exp(jax.random.uniform(streams_of[2], (D,), jnp.float32, math.log(0.29882812), math.log(3.0))), 0.29882812, 3.0).astype(jnp.bfloat16)
    residual = bell_draw(own_keys[3], (TOKENS, D), 1.0, 6.0, ((1, 16),))
    return dict(hidden=hidden, down_weight=down_weight, scales=scales, residual=residual)


def sylvester(matrix_order):
    row_ids = lax.broadcasted_iota(jnp.int32, (matrix_order, matrix_order), 0)
    col_ids = lax.broadcasted_iota(jnp.int32, (matrix_order, matrix_order), 1)
    common_bits = row_ids & col_ids
    parity = jnp.zeros((matrix_order, matrix_order), jnp.int32)
    for bit_level in range(max(matrix_order.bit_length() - 1, 0)):
        parity = parity + (common_bits >> bit_level & 1)
    return jnp.where(parity % 2 == 0, 1.0, -1.0).astype(jnp.float32)

def reference(hidden, down_weight, scales, residual):
    local_table = sylvester(LH) / math.sqrt(LH)
    cross_table = sylvester(N_TENSOR) / math.sqrt(N_TENSOR)
    grouped = hidden.astype(jnp.float32).reshape(TOKENS, N_TENSOR, FF // (N_TENSOR * LH), LH)
    turned = jnp.einsum('tsbc,cd->tsbd', grouped, local_table, precision=lax.Precision.HIGHEST)
    crossed = jnp.einsum('us,tsbd->tubd', cross_table, turned, precision=lax.Precision.HIGHEST)
    rotated = crossed.reshape(TOKENS, FF).astype(jnp.bfloat16)
    sums = jnp.dot(rotated, down_weight, preferred_element_type=jnp.float32)
    updated = residual.astype(jnp.float32) + scales.astype(jnp.float32)[None, :] * sums
    return updated.astype(jnp.bfloat16)
```

```python
import math

import jax
import jax.numpy as jnp
from jax import lax
from jax.experimental import pallas as pl
from jax.experimental.pallas import tpu as pltpu
from jax.sharding import PartitionSpec as P

LH = 64
WIDE = 256
CHUNKS = 4


def swap(x, axis, mask):
    return lax.ppermute(x, axis, [(i, i ^ mask) for i in range(lax.axis_size(axis))])


def sylvester(matrix_order):
    row_ids = lax.broadcasted_iota(jnp.int32, (matrix_order, matrix_order), 0)
    col_ids = lax.broadcasted_iota(jnp.int32, (matrix_order, matrix_order), 1)
    common_bits = row_ids & col_ids
    parity = jnp.zeros((matrix_order, matrix_order), jnp.int32)
    for bit_level in range(max(matrix_order.bit_length() - 1, 0)):
        parity = parity + (common_bits >> bit_level & 1)
    return jnp.where(parity % 2 == 0, 1.0, -1.0).astype(jnp.float32)


def any_size(hidden, down_weight, scales, residual):
    tensor_count = lax.axis_size("tensor")
    tok_rows, unit_count = hidden.shape
    local_table = sylvester(LH) / math.sqrt(LH)
    grouped = hidden.astype(jnp.float32).reshape(tok_rows, unit_count // LH, LH)
    current = jnp.einsum(
        "tbc,cd->tbd", grouped, local_table, precision=lax.Precision.HIGHEST
    ).reshape(tok_rows, unit_count)
    position = lax.axis_index("tensor")
    for bit_level in range(tensor_count.bit_length() - 1):
        partner = swap(current, "tensor", 1 << bit_level)
        upper_half = position >> bit_level & 1 == 1
        current = jnp.where(upper_half, partner - current, current + partner)
    rotated = (current * (1.0 / math.sqrt(tensor_count))).astype(jnp.bfloat16)
    out_cols = residual.shape[1]
    partial_cols = jnp.dot(
        lax.all_gather(rotated, "dp", axis=0, tiled=True),
        down_weight,
        preferred_element_type=jnp.float32,
    )
    owned_sums = lax.psum_scatter(partial_cols, "tensor", scatter_dimension=1, tiled=True)
    column = (lax.axis_index("dp") * tensor_count + position) * out_cols
    scale_cols = lax.dynamic_slice_in_dim(scales, column, out_cols).astype(jnp.float32)
    updated = residual.astype(jnp.float32) + scale_cols[None, :] * owned_sums
    return updated.astype(jnp.bfloat16)


def turn_kernel(own_table, table, a_ref, b_ref, r_ref, o_ref):
    for j in range(o_ref.shape[1] // WIDE):
        cols = slice(j * WIDE, (j + 1) * WIDE)
        acc = jnp.dot(a_ref[:, cols], own_table[...], preferred_element_type=jnp.float32)
        acc += jnp.dot(b_ref[:, cols], table[...], preferred_element_type=jnp.float32)
        acc += jnp.dot(r_ref[:, cols], table[...], preferred_element_type=jnp.float32)
        o_ref[:, cols] = acc.astype(o_ref.dtype)


def turn(own_table, table, a, b, r):
    rows, units = a.shape
    step = WIDE * next(n for n in (13, 8, 4, 2, 1) if units % (WIDE * n) == 0)
    whole = pl.BlockSpec((WIDE, WIDE), lambda i: (0, 0))
    part = pl.BlockSpec((rows, step), lambda i: (0, i))
    return pl.pallas_call(
        turn_kernel,
        grid=(units // step,),
        in_specs=[whole, whole, part, part, part],
        out_specs=part,
        out_shape=jax.ShapeDtypeStruct(a.shape, a.dtype),
        cost_estimate=pl.CostEstimate(
            flops=6 * rows * units * WIDE, bytes_accessed=8 * rows * units, transcendentals=0
        ),
    )(own_table, table, a, b, r)


def ring_of_four(hidden, down_weight, scales, residual):
    f32, bf16 = jnp.float32, jnp.bfloat16
    d = lax.axis_index("tensor")
    rank = lax.axis_index("dp")
    rows = hidden.shape[0]
    out_cols = residual.shape[1]
    odd = (d ^ d >> 1) & 1
    table = jnp.kron(jnp.eye(WIDE // LH, dtype=f32), sylvester(LH)) / 16.0
    own_sign = jnp.where(odd == 1, -1.0, 1.0)
    own_table = (table * own_sign).astype(bf16)
    table = table.astype(bf16)
    send_own = jnp.where(d >> 1 & 1 == 1, -1.0, 1.0)
    send_far = send_own * jnp.where(odd == 1, 1.0, -1.0)
    size = rows // CHUNKS

    def block(x, j):
        return lax.dynamic_slice_in_dim(x, j * out_cols, out_cols, 1)

    sums = []
    for k in range(CHUNKS):
        a = hidden[k * size : (k + 1) * size]
        b = swap(a, "tensor", 3)
        q = (send_own * a.astype(f32) + send_far * b.astype(f32)).astype(bf16)
        r = swap(q, "tensor", 1)
        rot = turn(own_table, table, a, b, r)
        far = swap(rot, "dp", 2)
        near = swap(rot, "dp", 1)
        both = swap(far, "dp", 1)
        tokens = jnp.concatenate([rot, near, far, both], axis=0)
        partial = jnp.dot(tokens, down_weight, preferred_element_type=f32)
        half = 2 * size
        done = []
        for rows_half, first, second in ((partial[:half], 3, 1), (partial[half:], 1, 3)):
            away = jnp.concatenate(
                [block(rows_half, d ^ first), block(rows_half, d ^ 2)], axis=1
            ).astype(bf16)
            back = swap(away, "tensor", first).astype(f32)
            onward = (block(rows_half, d ^ second) + back[:, out_cols:]).astype(bf16)
            last = swap(onward, "tensor", second).astype(f32)
            done.append(block(rows_half, d) + back[:, :out_cols] + last)
        sums.append(jnp.stack(done).reshape(4, size, out_cols))
    by_offset = jnp.concatenate(sums, axis=1)
    s0, s1, s2, s3 = by_offset
    low = rank & 1 == 1
    s0, s1 = jnp.where(low, s1, s0), jnp.where(low, s0, s1)
    s2, s3 = jnp.where(low, s3, s2), jnp.where(low, s2, s3)
    high = rank >> 1 & 1 == 1
    s0, s2 = jnp.where(high, s2, s0), jnp.where(high, s0, s2)
    s1, s3 = jnp.where(high, s3, s1), jnp.where(high, s1, s3)
    owned = jnp.concatenate([s0, s1, s2, s3], axis=0)
    column = (rank * 4 + d) * out_cols
    scale_cols = lax.dynamic_slice_in_dim(scales, column, out_cols).astype(f32)
    return (residual.astype(f32) + scale_cols[None, :] * owned).astype(bf16)


def shards(hidden, down_weight, scales, residual):
    fits = (
        lax.axis_size("tensor") == 4
        and lax.axis_size("dp") == 4
        and hidden.shape[0] % (16 * CHUNKS) == 0
        and hidden.shape[1] % WIDE == 0
    )
    return (ring_of_four if fits else any_size)(hidden, down_weight, scales, residual)


def solution(mesh):
    return jax.shard_map(
        shards,
        mesh=mesh,
        in_specs=(
            P(("groups", "dp"), "tensor"),
            P("tensor", "dp"),
            P(),
            P("groups", ("dp", "tensor")),
        ),
        out_specs=P("groups", ("dp", "tensor")),
        check_vma=False,
    )
```

```python
import math

import jax
import jax.numpy as jnp
from jax import lax
from jax.experimental import pallas as pl
from jax.experimental.pallas import tpu as pltpu
from jax.sharding import PartitionSpec as P

LH = 64
WIDE = 256
CHUNKS = (32, 32, 32, 32, 32, 32, 32, 16, 16)
LAG = 2
AHEAD = 2


def swap(x, axis, mask):
    return lax.ppermute(x, axis, [(i, i ^ mask) for i in range(lax.axis_size(axis))])


def sylvester(matrix_order):
    row_ids = lax.broadcasted_iota(jnp.int32, (matrix_order, matrix_order), 0)
    col_ids = lax.broadcasted_iota(jnp.int32, (matrix_order, matrix_order), 1)
    common_bits = row_ids & col_ids
    parity = jnp.zeros((matrix_order, matrix_order), jnp.int32)
    for bit_level in range(max(matrix_order.bit_length() - 1, 0)):
        parity = parity + (common_bits >> bit_level & 1)
    return jnp.where(parity % 2 == 0, 1.0, -1.0).astype(jnp.float32)


def any_size(hidden, down_weight, scales, residual):
    tensor_count = lax.axis_size("tensor")
    tok_rows, unit_count = hidden.shape
    local_table = sylvester(LH) / math.sqrt(LH)
    grouped = hidden.astype(jnp.float32).reshape(tok_rows, unit_count // LH, LH)
    current = jnp.einsum(
        "tbc,cd->tbd", grouped, local_table, precision=lax.Precision.HIGHEST
    ).reshape(tok_rows, unit_count)
    position = lax.axis_index("tensor")
    for bit_level in range(tensor_count.bit_length() - 1):
        partner = swap(current, "tensor", 1 << bit_level)
        upper_half = position >> bit_level & 1 == 1
        current = jnp.where(upper_half, partner - current, current + partner)
    rotated = (current * (1.0 / math.sqrt(tensor_count))).astype(jnp.bfloat16)
    out_cols = residual.shape[1]
    partial_cols = jnp.dot(
        lax.all_gather(rotated, "dp", axis=0, tiled=True),
        down_weight,
        preferred_element_type=jnp.float32,
    )
    owned_sums = lax.psum_scatter(partial_cols, "tensor", scatter_dimension=1, tiled=True)
    column = (lax.axis_index("dp") * tensor_count + position) * out_cols
    scale_cols = lax.dynamic_slice_in_dim(scales, column, out_cols).astype(jnp.float32)
    updated = residual.astype(jnp.float32) + scale_cols[None, :] * owned_sums
    return updated.astype(jnp.bfloat16)


def turn_kernel(signs, table, a_ref, near_ref, far_ref, last_ref, order_ref, own_ref, other_ref):
    rows = a_ref.shape[0]
    for j in range(a_ref.shape[1] // WIDE):
        cols = slice(j * WIDE, (j + 1) * WIDE)
        units = jnp.concatenate([ref[:, cols] for ref in (a_ref, near_ref, far_ref, last_ref)])
        turned = jnp.dot(units, table[...], preferred_element_type=jnp.float32)
        parts = [turned[i * rows : (i + 1) * rows] for i in range(4)]
        for u, out in enumerate((own_ref, other_ref)):
            total = signs[u, 0] * parts[0]
            for i in range(1, 4):
                total += signs[u, i] * parts[i]
            out[:, cols] = total.astype(out.dtype)


def turn(signs, table, a, near, far, last, order):
    rows, units = a.shape
    step = WIDE * next(n for n in (13, 8, 4, 2, 1) if units % (WIDE * n) == 0)
    part = pl.BlockSpec((rows, step), lambda i: (0, i))
    return pl.pallas_call(
        turn_kernel,
        grid=(units // step,),
        in_specs=[
            pl.BlockSpec(memory_space=pltpu.SMEM),
            pl.BlockSpec((WIDE, WIDE), lambda i: (0, 0)),
            part,
            part,
            part,
            part,
            pl.BlockSpec(memory_space=pl.ANY),
        ],
        out_specs=[part, part],
        out_shape=[jax.ShapeDtypeStruct(a.shape, a.dtype)] * 2,
        cost_estimate=pl.CostEstimate(
            flops=8 * rows * units * WIDE, bytes_accessed=12 * rows * units, transcendentals=0
        ),
    )(signs, table, a, near, far, last, order)


def down_kernel(t0, t1, t2, t3, weight_ref, order_ref, o_ref):
    @pl.when(pl.program_id(0) == 0)
    def _():
        o_ref[...] = jnp.zeros_like(o_ref)

    tokens = jnp.concatenate([t0[...], t1[...], t2[...], t3[...]])
    o_ref[...] += jnp.dot(tokens, weight_ref[...], preferred_element_type=jnp.float32)


def down(tokens, weight, order):
    rows, units = tokens[0].shape
    cols = weight.shape[1]
    step = next(n for n in (1024, 512, 256) if units % n == 0)
    part = pl.BlockSpec((rows, step), lambda i: (0, i))
    return pl.pallas_call(
        down_kernel,
        grid=(units // step,),
        in_specs=[part] * 4
        + [pl.BlockSpec((step, cols), lambda i: (i, 0)), pl.BlockSpec(memory_space=pl.ANY)],
        out_specs=pl.BlockSpec((4 * rows, cols), lambda i: (0, 0)),
        out_shape=jax.ShapeDtypeStruct((4 * rows, cols), jnp.float32),
        compiler_params=pltpu.CompilerParams(vmem_limit_bytes=32 * 1024 * 1024),
        cost_estimate=pl.CostEstimate(
            flops=8 * rows * units * cols, bytes_accessed=2 * units * cols, transcendentals=0
        ),
    )(*tokens, weight, order)


def after(x, other):
    return lax.optimization_barrier((x, other))[0]


def line_of_four(hidden, down_weight, scales, residual):
    f32, bf16 = jnp.float32, jnp.bfloat16
    d = lax.axis_index("tensor")
    rank = lax.axis_index("dp")
    out_cols = residual.shape[1]
    inner = (d ^ d >> 1) & 1 == 1
    table = (jnp.kron(jnp.eye(WIDE // LH, dtype=f32), sylvester(LH)) / 16.0).astype(bf16)

    def sign(u, s):
        both = u & s
        return jnp.where((both ^ both >> 1) & 1 == 1, -1.0, 1.0).astype(f32)

    signs = jnp.stack([jnp.stack([sign(u, d ^ m) for m in (0, 1, 3, 2)]) for u in (d, d ^ 1)])
    inward, across, outward = [(0, 1), (3, 2)], [(1, 2), (2, 1)], [(1, 0), (2, 3)]

    def block(x, j):
        return lax.dynamic_slice_in_dim(x, j * out_cols, out_cols, 1)

    starts = [sum(CHUNKS[:k]) * hidden.shape[0] // 256 for k in range(len(CHUNKS) + 1)]
    n = len(CHUNKS)
    gathered, turned, sums, partials = [None] * n, [None] * n, [None] * n, [None] * n
    order = table
    for k in range(n + LAG):
        if k < n:
            a = hidden[starts[k] : starts[k + 1]]
            if k >= AHEAD:
                a = after(a, turned[k - AHEAD])
            near = lax.ppermute(a, "tensor", inward)
            far = lax.ppermute(a, "tensor", across)
            last = lax.ppermute(near, "tensor", across)
            own, other = turn(signs, table, a, near, far, last, order)
            order = turned[k] = own
            rot = jnp.where(inner, own, lax.ppermute(other, "tensor", outward))
            x1 = swap(rot, "dp", 2)
            gathered[k] = [rot, swap(rot, "dp", 1), x1, swap(x1, "dp", 1)]
        j = k - LAG
        if j >= 0:
            partial = down(gathered[j], down_weight, order)
            order = partial
            away = jnp.concatenate([block(partial, d ^ 1), block(partial, d ^ 3)], axis=1)
            back = swap(away.astype(bf16), "tensor", 1).astype(f32)
            onward = (block(partial, d ^ 2) + back[:, out_cols:]).astype(bf16)
            final = swap(onward, "tensor", 2).astype(f32)
            done = block(partial, d) + back[:, :out_cols] + final
            sums[j] = done.reshape(4, done.shape[0] // 4, out_cols)
    by_offset = jnp.concatenate(sums, axis=1)
    s0, s1, s2, s3 = by_offset
    low = rank & 1 == 1
    s0, s1 = jnp.where(low, s1, s0), jnp.where(low, s0, s1)
    s2, s3 = jnp.where(low, s3, s2), jnp.where(low, s2, s3)
    high = rank >> 1 & 1 == 1
    s0, s2 = jnp.where(high, s2, s0), jnp.where(high, s0, s2)
    s1, s3 = jnp.where(high, s3, s1), jnp.where(high, s1, s3)
    owned = jnp.concatenate([s0, s1, s2, s3], axis=0)
    column = (rank * 4 + d) * out_cols
    scale_cols = lax.dynamic_slice_in_dim(scales, column, out_cols).astype(f32)
    return (residual.astype(f32) + scale_cols[None, :] * owned).astype(bf16)


def shards(hidden, down_weight, scales, residual):
    fits = (
        lax.axis_size("tensor") == 4
        and lax.axis_size("dp") == 4
        and hidden.shape[0] % 256 == 0
        and hidden.shape[1] % WIDE == 0
    )
    return (line_of_four if fits else any_size)(hidden, down_weight, scales, residual)


def solution(mesh):
    return jax.shard_map(
        shards,
        mesh=mesh,
        in_specs=(
            P(("groups", "dp"), "tensor"),
            P("tensor", "dp"),
            P(),
            P("groups", ("dp", "tensor")),
        ),
        out_specs=P("groups", ("dp", "tensor")),
        check_vma=False,
    )
```
